1024 devices in a mesh: node: 64 (over z, core), local: 16 (over x, y).
Axes of the slice: x: 4, y: 4, z: 32, core: 2. Of those that a mesh axis runs over, the one named last changes fastest.
Arguments:
- hidden_in: bfloat16 [4096, 7168], P('node', 'local'), may hold values from -6 to 6
- expert_ids: int32 [4096, 4], P('node'), may hold values from 0 to 63, all different within a row; in each aligned block of 64 rows (0 to 63, 64 to 127, ...) at most 8 rows name the same one
- gate_weights: float32 [4096, 4], P('node'), may hold values from 0.1 to 0.9
- w_in: bfloat16 [64, 7168, 2048], P('node', None, 'local'), may hold values from -0.0625 to 0.0625
- w_down: bfloat16 [64, 1024, 7168], P('node', None, 'local'), may hold values from -0.1875 to 0.1875
Outputs:
- mixed: bfloat16 [4096, 7168], P('node', 'local')
The draws below stay inside these ranges and needn't reach their ends.
Inputs may be any that keep to these rules, and one draw needn't show every extreme that they name: `expert_ids`: each token names 4 different experts. Among the tokens of one node group no expert is named more than 8 times, and in every draw some expert is named exactly 8 times by some group.
All inputs are finite; a program needn't handle non-finite values.
Results may differ from the reference program's by a relative error of at most 0.0057.
Values may be sent and summed in bfloat16 or wider, within the bound.
No kernel may reach another device: no remote copies, remote signals or barrier semaphores. Data moves between devices by JAX's collectives and lax.ppermute only.
A program may use at most 64 MiB of HBM per device.

```python
import math
import jax
import jax.numpy as jnp
import numpy as np
from jax import lax

D = 7168
HID = 1024
TOPK = 4
TOK_NODE = 64
EXPERTS = 64
CAP = 8
HU = 64
TOKENS = 4096
N_NODE = 64
N_LOCAL = 16


def shard_levels(key, extent, pieces, smallest, top_value):
    gain, own = 1.0, jax.random.fold_in(key, 6)
    for dim, shards_of in pieces:
        heights = jnp.exp(jax.random.uniform(jax.random.fold_in(own, dim), (shards_of,), jnp.float32, smallest / len(pieces), top_value / len(pieces)))
        gain = gain * jnp.repeat(heights, extent[dim] // shards_of).reshape([-1 if axis == dim else 1 for axis in range(len(extent))])
    return gain


def deal_out(rng, own, number, rows, amount, top, reach, skew):
    sequence = jax.random.permutation(rng, amount)
    heavy_load, common = portions_of(amount, rows * top, reach, skew, True), portions_of(amount, rows * top, reach, skew, False)
    places = jnp.arange(amount)

    def named(tallies, rotation):
        used = int((tallies > 0).sum())
        fixed = max(1, used // 4)
        shifted = fixed + (places - fixed + rotation * (used - fixed)) % max(1, amount - fixed)
        return jnp.zeros((amount,), jnp.int32).at[sequence[jnp.where(places < fixed, places, shifted)]].set(jnp.asarray(tallies, jnp.int32))

    tallies = jnp.where(number % 4 == 0, named(heavy_load, number // 4), named(common, number - number // 4 - 1))
    mixed = jax.random.permutation(jax.random.fold_in(own, 3), amount)
    giver, taker = mixed[0:amount // 2 * 2:2], mixed[1:amount // 2 * 2:2]
    margin = jnp.minimum(tallies[giver] - 1, reach - tallies[taker]) // 2
    margin = jnp.where((giver == sequence[0]) | (taker == sequence[0]) | (tallies[taker] == 0), 0, jnp.maximum(margin, 0))
    shifted = jax.random.randint(jax.random.fold_in(own, 4), (amount // 2,), 0, 1 << 20) % (margin + 1)
    tallies = tallies.at[giver].add(-shifted).at[taker].add(shifted)
    labels = jnp.searchsorted(jnp.cumsum(tallies), jnp.arange(rows * top), side="right").astype(jnp.int32)
    listing = labels.reshape(top, rows).T
    listing = listing[jax.random.permutation(jax.random.fold_in(own, 1), rows)]
    rotation = jax.random.randint(jax.random.fold_in(own, 2), (rows, 1), 0, top)
    return jnp.take_along_axis(listing, (jnp.arange(top)[None, :] + rotation) % top, axis=1)


def portions_of(number_of, total, limit, skew, full):
    portions = [(1 << 20) // math.isqrt(grade ** skew) + 1 for grade in range(1, number_of + 1)]
    largest = limit if full else min(limit, max(-(-total // number_of), total * portions[0] // sum(portions)))
    least = 1 if total - largest >= number_of - 1 else 0
    holding, rest = [largest] + [least] * (number_of - 1), total - largest - least * (number_of - 1)
    while rest > 0:
        candidates = [i for i in range(1, number_of) if holding[i] < largest] or [i for i in range(1, number_of) if holding[i] < limit]
        whole, left = sum([portions[i] for i in candidates]), rest
        for i in candidates:
            addition = min(limit - holding[i], max(1, left * portions[i] // whole), rest)
            holding[i] = holding[i] + addition
            rest = rest - addition
    return np.array(holding)


def normal_values(stream_key, dims, deviation, limit, cuts=(), held_as=jnp.bfloat16):
    loudness = shard_levels(stream_key, dims, cuts, -0.22, 0.18) if cuts else 1.0
    values = jax.random.normal(stream_key, dims, jnp.float32) * deviation * loudness
    return jnp.minimum(jnp.maximum(values, -limit), limit).astype(held_as)


def setup_inputs(seed: int = 0) -> dict:
    seeds = jax.random.split(jax.random.key(seed), 6)
    hidden_in = normal_values(seeds[0], (TOKENS, D), 1.0, 6.0, ((0, 64), (1, 16)))
    expert_ids_keys = jax.random.split(jax.random.fold_in(seeds[1], 1), TOKENS // TOK_NODE)
    expert_ids_turns = jax.random.permutation(jax.random.fold_in(seeds[1], 3), TOKENS // TOK_NODE)
    expert_ids = jax.vmap(lambda own, number: deal_out(jax.random.fold_in(seeds[1], 2), own, number, TOK_NODE, EXPERTS, TOPK, CAP, 2))(expert_ids_keys, expert_ids_turns).reshape((TOKENS, TOPK))
    gate_weights = jnp.clip(0.1 + 0.79999997 * jax.random.uniform(seeds[2], (TOKENS, TOPK), jnp.float32) ** shard_levels(seeds[2], (TOKENS, TOPK), ((0, 64),), -0.2, 0.2), 0.1, 0.9)
    w_in = normal_values(seeds[3], (EXPERTS, D, 2 * HID), D ** -0.5, 0.0625, ((0, 64), (2, 16)))
    w_down = normal_values(seeds[4], (EXPERTS, HID, D), HID ** -0.5, 0.1875, ((0, 64), (2, 16)))
    return dict(hidden_in=hidden_in, expert_ids=expert_ids, gate_weights=gate_weights, w_in=w_in, w_down=w_down)


def run_expert(args):
    rows, w_one, w_two = args
    flat = rows.reshape(N_NODE * CAP, D)
    projected = jnp.dot(flat, w_one, preferred_element_type=jnp.float32)
    split = projected.reshape(N_NODE * CAP, N_LOCAL, 2, HU)
    gate_part = split[:, :, 0, :].reshape(N_NODE * CAP, HID)
    up_part = split[:, :, 1, :].reshape(N_NODE * CAP, HID)
    activated = (jax.nn.silu(gate_part) * up_part).astype(jnp.bfloat16)
    result = jnp.dot(activated, w_two, preferred_element_type=jnp.float32).astype(jnp.bfloat16)
    return result.reshape(N_NODE, CAP, D)


def reference(hidden_in, expert_ids, gate_weights, w_in, w_down):
    routes = expert_ids.reshape(N_NODE, TOK_NODE * TOPK)
    onehot = (routes[:, :, None] == jnp.arange(EXPERTS, dtype=jnp.int32)[None, None, :]).astype(jnp.int32)
    earlier = jnp.cumsum(onehot, axis=1) - onehot
    slot_of = jnp.sum(earlier * onehot, axis=2).reshape(TOKENS, TOPK).astype(jnp.int32)
    group_of = (jnp.arange(TOKENS, dtype=jnp.int32) // TOK_NODE).astype(jnp.int32)
    group_of = jnp.broadcast_to(group_of[:, None], (TOKENS, TOPK))
    repeated = jnp.broadcast_to(hidden_in[:, None, :], (TOKENS, TOPK, D))
    buffers = jnp.zeros((EXPERTS, N_NODE, CAP, D), hidden_in.dtype)
    buffers = buffers.at[expert_ids, group_of, slot_of].set(repeated)
    outputs = lax.map(run_expert, (buffers, w_in, w_down))
    chosen = outputs[expert_ids, group_of, slot_of].astype(jnp.float32)
    mixed = jnp.sum(gate_weights[:, :, None] * chosen, axis=1)
    return mixed.astype(jnp.bfloat16)
```

```python
import jax
import jax.numpy as jnp
from jax import lax
from jax.sharding import Mesh, PartitionSpec as P

FAR = 4


def split_float(values):
    high = lax.reduce_precision(values, 8, 7)
    rest = values - high
    middle = lax.reduce_precision(rest, 8, 7)
    return [high, middle, rest - middle]


def route_tables(ids, pieces, near, capacity):
    tok_count = ids.shape[1]
    width = near * capacity
    lane = jnp.arange(width, dtype=jnp.int32)
    expert = lax.axis_index("far") * near + lane // capacity
    named = [ids[:, :, k, None] == expert for k in range(ids.shape[2])]
    chosen = sum(hit.astype(jnp.float32) for hit in named)
    order = jnp.arange(tok_count, dtype=jnp.int32)
    before = (order[None, :] < order[:, None]).astype(jnp.bfloat16)
    slot = jnp.einsum(
        "tu,guj->gtj", before, chosen.astype(jnp.bfloat16), preferred_element_type=jnp.float32
    )
    placed = (slot == (lane % capacity).astype(jnp.float32)) & (chosen > 0)
    select = placed.astype(jnp.bfloat16)
    combine = []
    for piece in pieces:
        weight = sum(
            jnp.where(hit, piece[:, :, k, None], 0.0) for k, hit in enumerate(named)
        )
        combine.append(jnp.where(placed, weight, 0.0).astype(jnp.bfloat16))
    return select, combine


def spread(block, axis):
    size = lax.axis_size(axis)
    copies = jnp.broadcast_to(block[None], (size, *block.shape))
    return lax.all_to_all(copies, axis, split_axis=0, concat_axis=0, tiled=True)


def local(hidden_in, expert_ids, gate_weights, w_in, w_down):
    far, near, parts = lax.axis_size("far"), lax.axis_size("near"), lax.axis_size("local")
    tok_count, features = hidden_in.shape
    top_count = expert_ids.shape[1]
    capacity = max(2, (2 * tok_count * top_count + far * near - 1) // (far * near))
    rows = far * near * capacity
    columns = w_in.shape[2]

    weights = lax.all_to_all(
        w_in.reshape(parts, features, columns), "local", split_axis=0, concat_axis=0, tiled=True
    )

    routing = [expert_ids.astype(jnp.float32)] + split_float(gate_weights)
    routing = jnp.concatenate(routing, axis=1).astype(jnp.bfloat16)
    payload = jnp.concatenate([hidden_in, routing], axis=1)
    gathered = spread(payload, "far")
    tokens = gathered[:, :, :features]
    routing = gathered[:, :, features:].astype(jnp.float32)
    ids = routing[:, :, :top_count].astype(jnp.int32)
    pieces = [routing[:, :, k * top_count : (k + 1) * top_count] for k in (1, 2, 3)]
    select, combine = route_tables(ids, pieces, near, capacity)

    outgoing = jnp.einsum(
        "gtj,gtd->gjd", select, tokens, preferred_element_type=jnp.float32
    ).astype(jnp.bfloat16)
    outgoing = outgoing.reshape(far, near, capacity, features).transpose(1, 0, 2, 3)
    arrived = lax.all_to_all(outgoing, "near", split_axis=0, concat_axis=0, tiled=True)
    arrived = arrived.reshape(rows, features)

    partial = jnp.einsum(
        "rd,ldj->lrj", arrived, weights, preferred_element_type=jnp.float32
    ).astype(jnp.bfloat16)
    partial = lax.all_to_all(partial, "local", split_axis=0, concat_axis=0, tiled=True)
    projected = jnp.sum(partial.astype(jnp.float32), axis=0)
    gate_part = projected[:, : columns // 2]
    up_part = projected[:, columns // 2 :]
    activated = (jax.nn.silu(gate_part) * up_part).astype(jnp.bfloat16)
    activated = spread(activated.T, "local").reshape(-1, rows)

    expert_out = lax.dot_general(
        activated, w_down[0], (((0,), (0,)), ((), ())), preferred_element_type=jnp.float32
    ).astype(jnp.bfloat16)
    returned = lax.all_to_all(
        expert_out.reshape(near, far, capacity, features),
        "near",
        split_axis=0,
        concat_axis=0,
        tiled=True,
    )
    returned = returned.transpose(1, 0, 2, 3).reshape(far, near * capacity, features)
    blocks = sum(
        jnp.einsum("gtj,gjd->gtd", piece, returned, preferred_element_type=jnp.float32)
        for piece in combine
    ).astype(jnp.bfloat16)
    blocks = lax.all_to_all(blocks, "far", split_axis=0, concat_axis=0, tiled=True)
    return jnp.sum(blocks.astype(jnp.float32), axis=0).astype(jnp.bfloat16)


def solution(mesh):
    node, parts = mesh.devices.shape
    split = Mesh(mesh.devices.reshape(FAR, node // FAR, parts), ("far", "near", "local"))
    nodes = ("far", "near")
    in_specs = (
        P(nodes, "local"),
        P(nodes, None),
        P(nodes, None),
        P(nodes, None, "local"),
        P(nodes, None, "local"),
    )
    out_specs = P(nodes, "local")
    return jax.shard_map(
        local, mesh=split, in_specs=in_specs, out_specs=out_specs, check_vma=False
    )
```

```python
import jax
import jax.numpy as jnp
from jax import lax
from jax.sharding import Mesh, PartitionSpec as P

FAR = 4
MID = 2
NODES = ("far", "mid", "near")


def split_float(values):
    high = lax.reduce_precision(values, 8, 7)
    rest = values - high
    middle = lax.reduce_precision(rest, 8, 7)
    return [high, middle, rest - middle]


def route_masks(ids, first, experts, capacity):
    tok_count, top_count = ids.shape[-2:]
    lane = jnp.arange(experts * capacity, dtype=jnp.int32)
    expert = first + lane // capacity
    named = [ids[..., k, None] == expert for k in range(top_count)]
    chosen = named[0]
    for hit in named[1:]:
        chosen = chosen | hit
    order = jnp.arange(tok_count, dtype=jnp.int32)
    before = (order[None, :] < order[:, None]).astype(jnp.bfloat16)
    slot = jnp.einsum(
        "tu,...uj->...tj", before, chosen.astype(jnp.bfloat16), preferred_element_type=jnp.float32
    )
    placed = chosen & (slot == (lane % capacity).astype(jnp.float32))
    return named, placed


def swap(blocks, axis):
    return lax.all_to_all(blocks, axis, split_axis=0, concat_axis=0, tiled=True)


def spread(block, axis):
    size = lax.axis_size(axis)
    return swap(jnp.broadcast_to(block[None], (size, *block.shape)), axis)


def local(hidden_in, expert_ids, gate_weights, w_in, w_down):
    far, mid, near = (lax.axis_size(axis) for axis in NODES)
    parts = lax.axis_size("local")
    tok_count, features = hidden_in.shape
    top_count = expert_ids.shape[1]
    nodes = far * mid * near
    capacity = max(2, (2 * tok_count * top_count + nodes - 1) // nodes)
    rows = nodes * capacity
    columns = w_in.shape[2]
    block = lax.axis_index("far") * mid + lax.axis_index("mid")

    weights = swap(w_in.reshape(parts, features, columns), "local")

    routing = [expert_ids.astype(jnp.float32)] + split_float(gate_weights)
    routing = jnp.concatenate(routing, axis=1).astype(jnp.bfloat16)
    payload = jnp.concatenate([hidden_in, routing], axis=1)
    gathered = lax.all_gather(payload, ("far", "mid"), axis=0)
    routing = gathered[:, :, features:]
    ids = routing[:, :, :top_count].astype(jnp.int32)

    _, placed = route_masks(ids, block * near, near, capacity)
    outgoing = jnp.einsum(
        "gtj,gtd->gjd",
        placed.astype(jnp.bfloat16),
        gathered[:, :, :features],
        preferred_element_type=jnp.float32,
    ).astype(jnp.bfloat16)
    outgoing = outgoing.reshape(far * mid, near, capacity, features).transpose(1, 0, 2, 3)
    outgoing, weights = lax.optimization_barrier((outgoing, weights))
    arrived = swap(outgoing, "near").reshape(near, far, mid, capacity, features)
    arrived = arrived.transpose(2, 0, 1, 3, 4).reshape(rows, features)

    partial = jnp.einsum(
        "rd,ldj->lrj", arrived, weights, preferred_element_type=jnp.float32
    ).astype(jnp.bfloat16)
    projected = jnp.sum(swap(partial, "local").astype(jnp.float32), axis=0)
    gate_part = projected[:, : columns // 2]
    up_part = projected[:, columns // 2 :]
    activated = (jax.nn.silu(gate_part) * up_part).astype(jnp.bfloat16)
    activated = spread(activated.T, "local").reshape(-1, rows)

    expert_out = lax.dot_general(
        activated, w_down[0], (((0,), (0,)), ((), ())), preferred_element_type=jnp.float32
    ).astype(jnp.bfloat16)
    returned = swap(expert_out.reshape(mid * near, far, capacity, features), ("mid", "near"))
    returned = returned.transpose(1, 0, 2, 3).reshape(far, -1, features)

    routing = routing.reshape(far, mid, tok_count, -1)
    routing = lax.dynamic_index_in_dim(routing, lax.axis_index("mid"), 1, keepdims=False)
    ids = routing[:, :, :top_count].astype(jnp.int32)
    named, placed = route_masks(ids, lax.axis_index("far") * mid * near, mid * near, capacity)
    blocks = 0.0
    for piece in (1, 2, 3):
        gates = routing[:, :, piece * top_count : (piece + 1) * top_count]
        combine = sum(
            jnp.where(hit & placed, gates[:, :, k, None], 0) for k, hit in enumerate(named)
        )
        blocks += jnp.einsum("gtj,gjd->gtd", combine, returned, preferred_element_type=jnp.float32)
    blocks = swap(blocks.astype(jnp.bfloat16), "far")
    return jnp.sum(blocks.astype(jnp.float32), axis=0).astype(jnp.bfloat16)


def solution(mesh):
    node, parts = mesh.devices.shape
    split = mesh.devices.reshape(FAR, MID, node // (FAR * MID), parts)
    split = Mesh(split, (*NODES, "local"))
    in_specs = (
        P(NODES, "local"),
        P(NODES, None),
        P(NODES, None),
        P(NODES, None, "local"),
        P(NODES, None, "local"),
    )
    out_specs = P(NODES, "local")
    return jax.shard_map(
        local, mesh=split, in_specs=in_specs, out_specs=out_specs, check_vma=False
    )
```

```python
import jax
import jax.numpy as jnp
from jax import lax
from jax.sharding import Mesh, PartitionSpec as P

FAR = 4
MID = 2
NODES = ("far", "mid", "near")


def split_float(values):
    high = lax.reduce_precision(values, 8, 7)
    rest = values - high
    middle = lax.reduce_precision(rest, 8, 7)
    return [high, middle, rest - middle]


def route_masks(ids, first, experts, capacity):
    tok_count, top_count = ids.shape[-2:]
    lane = jnp.arange(experts * capacity, dtype=jnp.int32)
    expert = first + lane // capacity
    named = [ids[..., k, None] == expert for k in range(top_count)]
    chosen = named[0]
    for hit in named[1:]:
        chosen = chosen | hit
    order = jnp.arange(tok_count, dtype=jnp.int32)
    before = (order[None, :] < order[:, None]).astype(jnp.bfloat16)
    slot = jnp.einsum(
        "tu,...uj->...tj", before, chosen.astype(jnp.bfloat16), preferred_element_type=jnp.float32
    )
    placed = chosen & (slot == (lane % capacity).astype(jnp.float32))
    return named, placed


def swap(blocks, axis):
    return lax.all_to_all(blocks, axis, split_axis=0, concat_axis=0, tiled=True)


def spread(block, axis):
    size = lax.axis_size(axis)
    return swap(jnp.broadcast_to(block[None], (size, *block.shape)), axis)


def local(hidden_in, expert_ids, gate_weights, w_in, w_down):
    far, mid, near = (lax.axis_size(axis) for axis in NODES)
    parts = lax.axis_size("local")
    tok_count, features = hidden_in.shape
    top_count = expert_ids.shape[1]
    nodes = far * mid * near
    capacity = max(2, (2 * tok_count * top_count + nodes - 1) // nodes)
    rows = nodes * capacity
    columns = w_in.shape[2]
    block = lax.axis_index("far") * mid + lax.axis_index("mid")

    weights = swap(w_in.reshape(parts, features, columns), "local")

    routing = [expert_ids.astype(jnp.float32)] + split_float(gate_weights)
    routing = jnp.concatenate(routing, axis=1).astype(jnp.bfloat16)
    payload = jnp.concatenate([hidden_in, routing], axis=1)
    gathered = lax.all_gather(payload, ("far", "mid"), axis=0)
    gathered = jnp.roll(gathered, -lax.axis_index("far") * mid, axis=0)
    routing = gathered[:, :, features:]
    ids = routing[:, :, :top_count].astype(jnp.int32)

    _, placed = route_masks(ids, block * near, near, capacity)
    outgoing = jnp.einsum(
        "gtj,gtd->gjd",
        placed.astype(jnp.bfloat16),
        gathered[:, :, :features],
        preferred_element_type=jnp.float32,
    ).astype(jnp.bfloat16)
    outgoing = outgoing.reshape(far * mid, near, capacity, features).transpose(1, 0, 2, 3)
    outgoing, weights = lax.optimization_barrier((outgoing, weights))
    arrived = swap(outgoing, "near").reshape(near, far, mid, capacity, features)
    arrived = arrived.transpose(2, 0, 1, 3, 4).reshape(rows, features)

    partial = jnp.einsum(
        "rd,ldj->lrj", arrived, weights, preferred_element_type=jnp.float32
    ).astype(jnp.bfloat16)
    projected = jnp.sum(swap(partial, "local").astype(jnp.float32), axis=0)
    gate_part = projected[:, : columns // 2]
    up_part = projected[:, columns // 2 :]
    activated = (jax.nn.silu(gate_part) * up_part).astype(jnp.bfloat16)
    activated = spread(activated.T, "local").reshape(-1, rows)

    expert_out = lax.dot_general(
        activated, w_down[0], (((0,), (0,)), ((), ())), preferred_element_type=jnp.float32
    ).astype(jnp.bfloat16)
    expert_out = expert_out.reshape(mid * near, far, capacity, features)

    routing = routing.reshape(far, mid, tok_count, -1)
    routing = lax.dynamic_index_in_dim(routing, lax.axis_index("mid"), 1, keepdims=False)
    ids = routing[:, :, :top_count].astype(jnp.int32)
    named, placed = route_masks(ids, lax.axis_index("far") * mid * near, mid * near, capacity)
    combine = []
    for piece in (1, 2, 3):
        gates = routing[:, :, piece * top_count : (piece + 1) * top_count]
        combine.append(
            sum(jnp.where(hit & placed, gates[:, :, k, None], 0) for k, hit in enumerate(named))
        )

    returned = swap(expert_out, ("mid", "near")).transpose(1, 0, 2, 3)
    returned = returned.reshape(far, mid * near * capacity, features)

    def block_sums(first, last):
        return sum(
            jnp.einsum(
                "gtj,gjd->gtd",
                piece[first:last],
                returned[first:last],
                preferred_element_type=jnp.float32,
            )
            for piece in combine
        )

    away = block_sums(1, far).astype(jnp.bfloat16)
    sent = [
        lax.ppermute(away[step - 1], "far", [(i, (i + step) % far) for i in range(far)])
        for step in sorted(range(1, far), key=lambda step: -min(step, far - step))
    ]
    mixed = block_sums(0, 1)[0]
    for block in sent:
        mixed += block.astype(jnp.float32)
    return mixed.astype(jnp.bfloat16)


def solution(mesh):
    node, parts = mesh.devices.shape
    split = mesh.devices.reshape(FAR, MID, node // (FAR * MID), parts)
    split = Mesh(split, (*NODES, "local"))
    in_specs = (
        P(NODES, "local"),
        P(NODES, None),
        P(NODES, None),
        P(NODES, None, "local"),
        P(NODES, None, "local"),
    )
    out_specs = P(NODES, "local")
    return jax.shard_map(
        local, mesh=split, in_specs=in_specs, out_specs=out_specs, check_vma=False
    )
```

```python
import jax
import jax.numpy as jnp
from jax import lax
from jax.sharding import Mesh, PartitionSpec as P

FAR = 4
MID = 4
NODES = ("far", "mid", "near")


def split_float(values):
    high = lax.reduce_precision(values, 8, 7)
    rest = values - high
    middle = lax.reduce_precision(rest, 8, 7)
    return [high, middle, rest - middle]


def route_masks(ids, first, experts, capacity):
    tok_count, top_count = ids.shape[-2:]
    lane = jnp.arange(experts * capacity, dtype=jnp.int32)
    expert = first + lane // capacity
    named = [ids[..., k, None] == expert for k in range(top_count)]
    chosen = named[0]
    for hit in named[1:]:
        chosen = chosen | hit
    order = jnp.arange(tok_count, dtype=jnp.int32)
    before = (order[None, :] < order[:, None]).astype(jnp.bfloat16)
    slot = jnp.einsum(
        "tu,...uj->...tj", before, chosen.astype(jnp.bfloat16), preferred_element_type=jnp.float32
    )
    placed = chosen & (slot == (lane % capacity).astype(jnp.float32))
    return named, placed


def swap(blocks, axis):
    return lax.all_to_all(blocks, axis, split_axis=0, concat_axis=0, tiled=True)


def spread(block, axis):
    size = lax.axis_size(axis)
    return swap(jnp.broadcast_to(block[None], (size, *block.shape)), axis)


def local(hidden_in, expert_ids, gate_weights, w_in, w_down):
    far, mid, near = (lax.axis_size(axis) for axis in NODES)
    parts = lax.axis_size("local")
    tok_count, features = hidden_in.shape
    top_count = expert_ids.shape[1]
    nodes = far * mid * near
    capacity = max(2, (2 * tok_count * top_count + nodes - 1) // nodes)
    rows = nodes * capacity
    columns = w_in.shape[2]
    block = lax.axis_index("far") * mid + lax.axis_index("mid")

    weights = swap(w_in.reshape(parts, features, columns), "local")

    routing = [expert_ids.astype(jnp.float32)] + split_float(gate_weights)
    routing = jnp.concatenate(routing, axis=1).astype(jnp.bfloat16)
    payload = jnp.concatenate([hidden_in, routing], axis=1)
    gathered = lax.all_gather(payload, ("far", "mid"), axis=0)
    gathered = jnp.roll(gathered, -lax.axis_index("far") * mid, axis=0)
    routing = gathered[:, :, features:]
    ids = routing[:, :, :top_count].astype(jnp.int32)

    _, placed = route_masks(ids, block * near, near, capacity)
    outgoing = jnp.einsum(
        "gtj,gtd->gjd",
        placed.astype(jnp.bfloat16),
        gathered[:, :, :features],
        preferred_element_type=jnp.float32,
    ).astype(jnp.bfloat16)
    outgoing = outgoing.reshape(far * mid, near, capacity, features).transpose(1, 0, 2, 3)
    outgoing, weights = lax.optimization_barrier((outgoing, weights))
    arrived = swap(outgoing, "near").reshape(near, far, mid, capacity, features)
    arrived = arrived.transpose(2, 0, 1, 3, 4).reshape(rows, features)

    partial = jnp.einsum(
        "rd,ldj->lrj", arrived, weights, preferred_element_type=jnp.float32
    ).astype(jnp.bfloat16)
    projected = jnp.sum(swap(partial, "local").astype(jnp.float32), axis=0)
    gate_part = projected[:, : columns // 2]
    up_part = projected[:, columns // 2 :]
    activated = (jax.nn.silu(gate_part) * up_part).astype(jnp.bfloat16)
    activated = spread(activated.T, "local").reshape(-1, rows)

    expert_out = lax.dot_general(
        activated, w_down[0], (((0,), (0,)), ((), ())), preferred_element_type=jnp.float32
    ).astype(jnp.bfloat16)
    expert_out = expert_out.reshape(mid * near, far, capacity, features)

    routing = routing.reshape(far, mid, tok_count, -1)
    routing = lax.dynamic_index_in_dim(routing, lax.axis_index("mid"), 1, keepdims=False)
    ids = routing[:, :, :top_count].astype(jnp.int32)
    named, placed = route_masks(ids, lax.axis_index("far") * mid * near, mid * near, capacity)
    combine = []
    for piece in (1, 2, 3):
        gates = routing[:, :, piece * top_count : (piece + 1) * top_count]
        combine.append(
            sum(jnp.where(hit & placed, gates[:, :, k, None], 0) for k, hit in enumerate(named))
        )

    returned = swap(expert_out, ("mid", "near")).transpose(1, 0, 2, 3)
    returned = returned.reshape(far, mid * near * capacity, features)

    def block_sums(first, last):
        return sum(
            jnp.einsum(
                "gtj,gjd->gtd",
                piece[first:last],
                returned[first:last],
                preferred_element_type=jnp.float32,
            )
            for piece in combine
        )

    away = block_sums(1, far).astype(jnp.bfloat16)
    sent = [
        lax.ppermute(away[step - 1], "far", [(i, (i + step) % far) for i in range(far)])
        for step in sorted(range(1, far), key=lambda step: -min(step, far - step))
    ]
    mixed = block_sums(0, 1)[0]
    for block in sent:
        mixed += block.astype(jnp.float32)
    return mixed.astype(jnp.bfloat16)


def solution(mesh):
    node, parts = mesh.devices.shape
    split = mesh.devices.reshape(FAR, MID, node // (FAR * MID), parts)
    split = Mesh(split, (*NODES, "local"))
    in_specs = (
        P(NODES, "local"),
        P(NODES, None),
        P(NODES, None),
        P(NODES, None, "local"),
        P(NODES, None, "local"),
    )
    out_specs = P(NODES, "local")
    return jax.shard_map(
        local, mesh=split, in_specs=in_specs, out_specs=out_specs, check_vma=False
    )
```

```python
import jax
import jax.numpy as jnp
from jax import lax
from jax.sharding import Mesh, PartitionSpec as P

FAR = 4
MID = 4
LANES = 128
NODES = ("far", "mid", "near")


def split_float(values):
    high = lax.reduce_precision(values, 8, 7)
    rest = values - high
    middle = lax.reduce_precision(rest, 8, 7)
    return [high, middle, rest - middle]


def route_masks(ids, first, experts, capacity):
    tok_count, top_count = ids.shape[-2:]
    lane = jnp.arange(experts * capacity, dtype=jnp.int32)
    expert = first + lane // capacity
    named = [ids[..., k, None] == expert for k in range(top_count)]
    chosen = named[0]
    for hit in named[1:]:
        chosen = chosen | hit
    order = jnp.arange(tok_count, dtype=jnp.int32)
    before = (order[None, :] < order[:, None]).astype(jnp.bfloat16)
    slot = jnp.einsum(
        "tu,...uj->...tj", before, chosen.astype(jnp.bfloat16), preferred_element_type=jnp.float32
    )
    placed = chosen & (slot == (lane % capacity).astype(jnp.float32))
    return named, placed


def swap(blocks, axis):
    return lax.all_to_all(blocks, axis, split_axis=0, concat_axis=0, tiled=True)


def spread(block, axis):
    size = lax.axis_size(axis)
    return swap(jnp.broadcast_to(block[None], (size, *block.shape)), axis)


def pack(blocks):
    rows, features = blocks.shape[1:]
    whole = features // LANES
    parts = [blocks[:, :, k * LANES : (k + 1) * LANES] for k in range(whole)]
    rest = blocks[:, :, whole * LANES :]
    parts.append(jnp.concatenate([rest[:, : rows // 2], rest[:, rows // 2 :]], axis=2))
    return jnp.concatenate(parts, axis=1)


def unpack(packed, rows):
    whole = packed.shape[1] // rows
    parts = [packed[:, k * rows : (k + 1) * rows] for k in range(whole)]
    rest = packed[:, whole * rows :]
    parts.append(jnp.concatenate([rest[:, :, : LANES // 2], rest[:, :, LANES // 2 :]], axis=1))
    return jnp.concatenate(parts, axis=2)


def local(hidden_in, expert_ids, gate_weights, w_in, w_down):
    far, mid, near = (lax.axis_size(axis) for axis in NODES)
    parts = lax.axis_size("local")
    tok_count, features = hidden_in.shape
    top_count = expert_ids.shape[1]
    nodes = far * mid * near
    capacity = max(2, (2 * tok_count * top_count + nodes - 1) // nodes)
    rows = nodes * capacity
    columns = w_in.shape[2]
    block = lax.axis_index("far") * mid + lax.axis_index("mid")

    weights = swap(w_in.reshape(parts, features, columns), "local")

    routing = [expert_ids.astype(jnp.float32)] + split_float(gate_weights)
    routing = jnp.concatenate(routing, axis=1).astype(jnp.bfloat16)
    payload = jnp.concatenate([hidden_in, routing], axis=1)
    gathered = lax.all_gather(payload, ("far", "mid"), axis=0)
    gathered = jnp.roll(gathered, -lax.axis_index("far") * mid, axis=0)
    routing = gathered[:, :, features:]
    ids = routing[:, :, :top_count].astype(jnp.int32)

    _, placed = route_masks(ids, block * near, near, capacity)
    outgoing = jnp.einsum(
        "gtj,gtd->gjd",
        placed.astype(jnp.bfloat16),
        gathered[:, :, :features],
        preferred_element_type=jnp.float32,
    ).astype(jnp.bfloat16)
    outgoing = outgoing.reshape(far * mid, near, capacity, features).transpose(1, 0, 2, 3)
    outgoing, weights = lax.optimization_barrier((outgoing, weights))
    arrived = swap(outgoing, "near").reshape(near, far, mid, capacity, features)
    arrived = arrived.transpose(2, 0, 1, 3, 4).reshape(rows, features)

    partial = jnp.einsum(
        "rd,ldj->lrj", arrived, weights, preferred_element_type=jnp.float32
    ).astype(jnp.bfloat16)
    projected = jnp.sum(swap(partial, "local").astype(jnp.float32), axis=0)
    gate_part = projected[:, : columns // 2]
    up_part = projected[:, columns // 2 :]
    activated = (jax.nn.silu(gate_part) * up_part).astype(jnp.bfloat16)
    activated = spread(activated.T, "local").reshape(-1, rows)

    expert_out = lax.dot_general(
        activated, w_down[0], (((0,), (0,)), ((), ())), preferred_element_type=jnp.float32
    ).astype(jnp.bfloat16)
    expert_out = expert_out.reshape(mid * near, far, capacity, features)

    routing = routing.reshape(far, mid, tok_count, -1)
    routing = lax.dynamic_index_in_dim(routing, lax.axis_index("mid"), 1, keepdims=False)
    ids = routing[:, :, :top_count].astype(jnp.int32)
    named, placed = route_masks(ids, lax.axis_index("far") * mid * near, mid * near, capacity)
    combine = []
    for piece in (1, 2, 3):
        gates = routing[:, :, piece * top_count : (piece + 1) * top_count]
        combine.append(
            sum(jnp.where(hit & placed, gates[:, :, k, None], 0) for k, hit in enumerate(named))
        )

    returned = pack(expert_out.reshape(mid * near, far * capacity, features))
    returned = unpack(swap(returned, ("mid", "near")), far * capacity)
    returned = returned.reshape(mid * near, far, capacity, features).transpose(1, 0, 2, 3)
    returned = returned.reshape(far, mid * near * capacity, features)

    def block_sums(first, last):
        return sum(
            jnp.einsum(
                "gtj,gjd->gtd",
                piece[first:last],
                returned[first:last],
                preferred_element_type=jnp.float32,
            )
            for piece in combine
        )

    away = block_sums(1, far).astype(jnp.bfloat16)
    sent = [
        lax.ppermute(away[step - 1], "far", [(i, (i + step) % far) for i in range(far)])
        for step in sorted(range(1, far), key=lambda step: -min(step, far - step))
    ]
    mixed = block_sums(0, 1)[0]
    for block in sent:
        mixed += block.astype(jnp.float32)
    return mixed.astype(jnp.bfloat16)


def solution(mesh):
    node, parts = mesh.devices.shape
    split = mesh.devices.reshape(FAR, MID, node // (FAR * MID), parts)
    split = Mesh(split, (*NODES, "local"))
    in_specs = (
        P(NODES, "local"),
        P(NODES, None),
        P(NODES, None),
        P(NODES, None, "local"),
        P(NODES, None, "local"),
    )
    out_specs = P(NODES, "local")
    return jax.shard_map(
        local, mesh=split, in_specs=in_specs, out_specs=out_specs, check_vma=False
    )
```

```python
import jax
import jax.numpy as jnp
from jax import lax
from jax.sharding import Mesh, PartitionSpec as P

FAR = 4
MID = 4
LANES = 128
NODES = ("far", "mid", "near")


def split_float(values):
    high = lax.reduce_precision(values, 8, 7)
    rest = values - high
    middle = lax.reduce_precision(rest, 8, 7)
    return [high, middle, rest - middle]


def route_masks(ids, first, experts, capacity):
    tok_count, top_count = ids.shape[-2:]
    lane = jnp.arange(experts * capacity, dtype=jnp.int32)
    expert = first + lane // capacity
    named = [ids[..., k, None] == expert for k in range(top_count)]
    chosen = named[0]
    for hit in named[1:]:
        chosen = chosen | hit
    order = jnp.arange(tok_count, dtype=jnp.int32)
    before = (order[None, :] < order[:, None]).astype(jnp.bfloat16)
    slot = jnp.einsum(
        "tu,...uj->...tj", before, chosen.astype(jnp.bfloat16), preferred_element_type=jnp.float32
    )
    placed = chosen & (slot == (lane % capacity).astype(jnp.float32))
    return named, placed


def swap(blocks, axis):
    return lax.all_to_all(blocks, axis, split_axis=0, concat_axis=0, tiled=True)


def spread(block, axis):
    size = lax.axis_size(axis)
    return swap(jnp.broadcast_to(block[None], (size, *block.shape)), axis)


def pack(blocks):
    rows, features = blocks.shape[1:]
    whole = features // LANES
    parts = [blocks[:, :, k * LANES : (k + 1) * LANES] for k in range(whole)]
    rest = blocks[:, :, whole * LANES :]
    parts.append(jnp.concatenate([rest[:, : rows // 2], rest[:, rows // 2 :]], axis=2))
    return jnp.concatenate(parts, axis=1)


def unpack(packed, rows):
    whole = packed.shape[1] // rows
    parts = [packed[:, k * rows : (k + 1) * rows] for k in range(whole)]
    rest = packed[:, whole * rows :]
    parts.append(jnp.concatenate([rest[:, :, : LANES // 2], rest[:, :, LANES // 2 :]], axis=1))
    return jnp.concatenate(parts, axis=2)


def local(hidden_in, expert_ids, gate_weights, w_in, w_down):
    far, mid, near = (lax.axis_size(axis) for axis in NODES)
    parts = lax.axis_size("local")
    tok_count, features = hidden_in.shape
    top_count = expert_ids.shape[1]
    nodes = far * mid * near
    capacity = max(2, (2 * tok_count * top_count + nodes - 1) // nodes)
    rows = nodes * capacity
    columns = w_in.shape[2]
    block = lax.axis_index("far") * mid + lax.axis_index("mid")

    weights = swap(w_in.reshape(parts, features, columns), "local")

    routing = [expert_ids.astype(jnp.float32)] + split_float(gate_weights)
    routing = jnp.concatenate(routing, axis=1).astype(jnp.bfloat16)
    payload = jnp.concatenate([hidden_in, routing], axis=1)
    gathered = lax.all_gather(payload, ("far", "mid"), axis=0)
    gathered = jnp.roll(gathered, -lax.axis_index("far") * mid, axis=0)
    routing = gathered[:, :, features:]
    ids = routing[:, :, :top_count].astype(jnp.int32)

    _, placed = route_masks(ids, block * near, near, capacity)
    outgoing = jnp.einsum(
        "gtj,gtd->gjd",
        placed.astype(jnp.bfloat16),
        gathered[:, :, :features],
        preferred_element_type=jnp.float32,
    ).astype(jnp.bfloat16)
    outgoing = outgoing.reshape(far * mid, near, capacity, features).transpose(1, 0, 2, 3)
    outgoing, weights = lax.optimization_barrier((outgoing, weights))
    arrived = swap(outgoing, "near").reshape(near, far, mid, capacity, features)
    arrived = arrived.transpose(2, 0, 1, 3, 4).reshape(rows, features)

    partial = jnp.einsum(
        "rd,ldj->lrj", arrived, weights, preferred_element_type=jnp.float32
    ).astype(jnp.bfloat16)
    projected = jnp.sum(swap(partial, "local").astype(jnp.float32), axis=0)
    gate_part = projected[:, : columns // 2]
    up_part = projected[:, columns // 2 :]
    activated = (jax.nn.silu(gate_part) * up_part).astype(jnp.bfloat16)
    activated = spread(activated.T, "local").reshape(-1, rows)

    expert_out = lax.dot_general(
        activated, w_down[0], (((0,), (0,)), ((), ())), preferred_element_type=jnp.float32
    ).astype(jnp.bfloat16)
    expert_out = expert_out.reshape(mid * near, far, capacity, features)

    routing = routing.reshape(far, mid, tok_count, -1)
    routing = lax.dynamic_index_in_dim(routing, lax.axis_index("mid"), 1, keepdims=False)
    ids = routing[:, :, :top_count].astype(jnp.int32)
    named, placed = route_masks(ids, lax.axis_index("far") * mid * near, mid * near, capacity)
    combine = []
    for piece in (1, 2, 3):
        gates = routing[:, :, piece * top_count : (piece + 1) * top_count]
        combine.append(
            sum(jnp.where(hit & placed, gates[:, :, k, None], 0) for k, hit in enumerate(named))
        )

    returned = pack(expert_out.reshape(mid * near, far * capacity, features))
    returned = unpack(swap(returned, ("mid", "near")), far * capacity)
    returned = returned.reshape(mid * near, far, capacity, features).transpose(1, 0, 2, 3)
    returned = returned.reshape(far, mid * near * capacity, features)

    def block_sums(first, last):
        return sum(
            jnp.einsum(
                "gtj,gjd->gtd",
                piece[first:last],
                returned[first:last],
                preferred_element_type=jnp.float32,
            )
            for piece in combine
        )

    away = pack(block_sums(1, far).astype(jnp.bfloat16))
    sent = [
        lax.ppermute(away[step - 1], "far", [(i, (i + step) % far) for i in range(far)])
        for step in sorted(range(1, far), key=lambda step: -min(step, far - step))
    ]
    mixed = block_sums(0, 1)[0]
    for block in sent:
        mixed += unpack(block[None], tok_count)[0].astype(jnp.float32)
    return mixed.astype(jnp.bfloat16)


def solution(mesh):
    node, parts = mesh.devices.shape
    split = mesh.devices.reshape(FAR, MID, node // (FAR * MID), parts)
    split = Mesh(split, (*NODES, "local"))
    in_specs = (
        P(NODES, "local"),
        P(NODES, None),
        P(NODES, None),
        P(NODES, None, "local"),
        P(NODES, None, "local"),
    )
    out_specs = P(NODES, "local")
    return jax.shard_map(
        local, mesh=split, in_specs=in_specs, out_specs=out_specs, check_vma=False
    )
```
